32 devices in a mesh: ens: 2 (over x), region: 16 (over z, y, core).
Axes of the slice: x: 2, y: 2, z: 4, core: 2. Of those that a mesh axis runs over, the one named last changes fastest.
Arguments:
- velocity_start: float32 [2, 20, 16384], P(None, None, ('ens', 'region')), parts along dimension 2, may hold values from -6 to 6
- forcing: float32 [2, 20, 16384], P(None, None, ('ens', 'region')), parts along dimension 2, may hold values from -6 to 6
- rate_factor: float32 [20, 16384], P(None, ('ens', 'region')), parts along dimension 1, may hold values from 0.5 to 2
- basal_drag: float32 [8192], P('region'), may hold values from 0.1 to 10
- edge_weight: float32 [6, 8192], P(None, 'region'), may hold values from 0.3 to 1.5
- nbr_local: int32 [6, 8192], P(None, 'region'), may hold values from 0 to 575, as said below
- send_list: int32 [2, 512], P(None, 'region'), may hold values from 0 to 511, as said below
- ice_mask: int32 [8192], P('region'), may hold values from 0 to 1, as said below
Outputs:
- velocity: float32 [2, 20, 16384], P(None, None, ('ens', 'region')), parts along dimension 2
- newton_residual: float32 [2, 20, 16384], P(None, None, ('ens', 'region')), parts along dimension 2
The draws below stay inside these ranges and needn't reach their ends.
There are 2 independent parts, one for each index of `ens`. The reference program is written for one: setup_inputs(seed, part) draws one part's arguments, and reference() takes and returns one part's arrays. A program takes and returns all parts, laid end to end along the dimension named above; an argument that names none is the same for every part. Nothing has to cross between parts.
Inputs may be any that keep to these rules, and one draw needn't show every extreme that they name: `nbr_local`: column c of a partition (c = 0, ..., 511) has its neighbours within 32 positions of its own position 32 + c in the extended list, so only columns near a partition's ends reach the halo blocks. `send_list`: a partition sends each of its first 32 columns once to the lower neighbour and each of its last 32 columns once to the upper one. `ice_mask`: each partition holds between a quarter of 512 and 384 ice columns, and some partition holds exactly 384.
All inputs are finite; a program needn't handle non-finite values.
Results may differ from the reference program's by a relative error of at most 0.0003.
Values sent between devices are 32-bit elements; how exact they have to be, the bound alone decides.
A program may use at most 64 MiB of HBM per device.

```python
import math
import jax
import jax.numpy as jnp
from jax import lax

COL_DEV = 512
L = 20
NB = 6
M = 4
SWEEPS = 3
HB = 32
CAP = 384
NCOL = 8192
N_REGION = 16


def draw_ice_mask(key, part):
    key = jax.random.fold_in(key, 11)
    key_count, key_full, key_order = jax.random.split(key, 3)
    counts = jax.random.randint(key_count, (N_REGION,), COL_DEV // 4, CAP + 1)
    fullest = jax.random.randint(key_full, (), 0, N_REGION)
    counts = jnp.where(jnp.arange(N_REGION) == fullest, CAP, counts)
    inner_count = COL_DEV - 2 * HB
    orders = jax.vmap(lambda sub: jax.random.permutation(sub, inner_count))(jax.random.split(key_order, N_REGION))
    inner = (orders < counts[:, None] - 2 * HB).astype(jnp.int32)
    ends = jnp.ones((N_REGION, HB), jnp.int32)
    return jnp.concatenate([ends, inner, ends], axis=1).reshape(-1)


def draw_send_list(key, part):
    key = jax.random.fold_in(key, 5)
    orders = jax.vmap(lambda sub: jax.random.permutation(sub, HB))(jax.random.split(key, N_REGION)).astype(jnp.int32)
    to_lower = orders.reshape(-1)
    to_upper = (COL_DEV - 1 - orders).reshape(-1)
    return jnp.stack([to_lower, to_upper], axis=0).astype(jnp.int32)


def draw_nbr_local(key, part):
    key = jax.random.fold_in(key, 7)
    key_off, key_rim = jax.random.split(key)
    offsets = jax.random.randint(key_off, (NB, NCOL), -HB, HB + 1)
    spread = jax.random.randint(key_rim, (NB, NCOL), 0, HB)
    local_col = (jnp.arange(NCOL, dtype=jnp.int32) % COL_DEV)[None, :]
    which = jnp.arange(NB, dtype=jnp.int32)[:, None]
    places = jnp.clip(HB + local_col + offsets, 0, COL_DEV + 2 * HB - 1)
    low_room = jnp.maximum(HB - local_col, 1)
    low_place = local_col + spread % low_room
    places = jnp.where((which < 3) & (local_col < HB), low_place, places)
    high_room = jnp.maximum(HB + local_col - COL_DEV + 1, 1)
    high_place = HB + COL_DEV + spread % high_room
    places = jnp.where((which >= 3) & (local_col >= COL_DEV - HB), high_place, places)
    places = jnp.where((which == 0) & (local_col == 0), 0, places)
    places = jnp.where((which == 3) & (local_col == COL_DEV - 1), COL_DEV + 2 * HB - 1, places)
    return places.astype(jnp.int32)


def block_levels(stream_key, shape, cuts, low, largest):
    level, own = 1.0, jax.random.fold_in(stream_key, 6)
    for position, parts in cuts:
        draws = jnp.exp(jax.random.uniform(jax.random.fold_in(own, position), (parts,), jnp.float32, low / len(cuts), largest / len(cuts)))
        level = level * jnp.repeat(draws, shape[position] // parts).reshape([-1 if axis == position else 1 for axis in range(len(shape))])
    return level


def scatter_about(rng, extent, scale, bound, shards=(), kind=jnp.bfloat16):
    factor_of = block_levels(rng, extent, shards, -0.22, 0.18) if shards else 1.0
    result = jax.random.normal(rng, extent, jnp.float32) * scale * factor_of
    return jnp.minimum(jnp.maximum(result, -bound), bound).astype(kind)


def setup_inputs(seed: int = 0, part: int = 0) -> dict:
    streams_of = jax.random.split(jax.random.key(seed), 9)
    own_keys = jax.random.split(jax.random.fold_in(streams_of[8], part), 9)
    return {
        "velocity_start": scatter_about(own_keys[0], (2, L, NCOL), 1.0, 6.0, ((2, 16),), jnp.float32),
        "forcing": scatter_about(own_keys[1], (2, L, NCOL), 1.0, 6.0, ((2, 16),), jnp.float32),
        "rate_factor": jnp.clip(jnp.exp(math.log(2.0) - 1.3862944 * jax.random.uniform(own_keys[2], (L, NCOL), jnp.float32) ** block_levels(own_keys[2], (L, NCOL), ((1, 16),), -0.2, 0.2)), 0.5, 2.0),
        "basal_drag": jnp.clip(jnp.exp(math.log(10.0) - 4.6051702 * jax.random.uniform(streams_of[3], (NCOL,), jnp.float32) ** block_levels(streams_of[3], (NCOL,), ((0, 16),), -0.2, 0.2)), 0.1, 10.0),
        "edge_weight": jnp.clip(jnp.exp(math.log(1.5) - 1.60943787 * jax.random.uniform(streams_of[4], (NB, NCOL), jnp.float32) ** block_levels(streams_of[4], (NB, NCOL), ((1, 16),), -0.2, 0.2)), 0.3, 1.5),
        "nbr_local": draw_nbr_local(jax.random.fold_in(streams_of[8], 71), part),
        "send_list": draw_send_list(jax.random.fold_in(streams_of[8], 71), part),
        "ice_mask": draw_ice_mask(jax.random.fold_in(streams_of[8], 71), part),
    }


def extend(field, send_list):
    lead = field.shape[:-1]
    grid = field.reshape(lead + (N_REGION, COL_DEV))
    sends = send_list.reshape(2, N_REGION, HB)
    to_lower = jnp.take_along_axis(grid, jnp.broadcast_to(sends[0], lead + (N_REGION, HB)), axis=-1)
    to_upper = jnp.take_along_axis(grid, jnp.broadcast_to(sends[1], lead + (N_REGION, HB)), axis=-1)
    blank = jnp.zeros(lead + (1, HB), jnp.float32)
    lower_rim = jnp.concatenate([blank, to_upper[..., :-1, :]], axis=-2)
    upper_rim = jnp.concatenate([to_lower[..., 1:, :], blank], axis=-2)
    return jnp.concatenate([lower_rim, grid, upper_rim], axis=-1)

def neighbours(field, send_list, nbr_local, edge_weight):
    lead = field.shape[:-1]
    extended = extend(field, send_list)
    places = nbr_local.reshape(NB, N_REGION, COL_DEV)
    weights = edge_weight.reshape(NB, N_REGION, COL_DEV)
    total = jnp.zeros(lead + (N_REGION, COL_DEV), jnp.float32)
    for which in range(NB):
        picked = jnp.take_along_axis(extended, jnp.broadcast_to(places[which], lead + (N_REGION, COL_DEV)), axis=-1)
        total = total + weights[which] * picked
    return total.reshape(lead + (NCOL,))

def viscosity_of(velocity_start, rate_factor):
    steps_up = velocity_start[:, 1:] - velocity_start[:, :-1]
    steps_up = jnp.concatenate([steps_up, jnp.zeros_like(velocity_start[:, :1])], axis=1)
    shear = lax.optimization_barrier(jnp.sum(steps_up * steps_up, axis=0))
    return rate_factor * (1.0 + shear) ** (-1.0 / 3.0)

def local_terms(field, viscosity, face_visc, weight_total, basal_drag):
    flux = face_visc * (field[:, 1:] - field[:, :-1])
    blank = jnp.zeros_like(field[:, :1])
    vertical = -4.0 * (jnp.concatenate([flux, blank], axis=1) - jnp.concatenate([blank, flux], axis=1))
    bed = jnp.concatenate([(basal_drag * field[:, 0])[:, None], jnp.zeros_like(field[:, 1:])], axis=1)
    return vertical + (weight_total + 1.0) * viscosity * field + bed

def band_terms(viscosity, face_visc, weight_total, basal_drag, iced):
    blank = jnp.zeros_like(viscosity[:1])
    upper = jnp.concatenate([-4.0 * face_visc, blank], axis=0)
    lower = jnp.concatenate([blank, -4.0 * face_visc], axis=0)
    bottom = jnp.concatenate([basal_drag[None], jnp.zeros_like(viscosity[1:])], axis=0)
    middle = -upper - lower + (weight_total + 1.0) * viscosity + bottom
    return (lower * iced, iced * middle + (1.0 - iced), upper * iced)

def thomas(lower, middle, upper, right):
    layers = middle.shape[0]
    primes = [upper[0] / middle[0]]
    values = [right[:, 0] / middle[0]]
    for layer in range(1, layers):
        denom = middle[layer] - lower[layer] * primes[layer - 1]
        primes.append(upper[layer] / denom)
        values.append((right[:, layer] - lower[layer] * values[layer - 1]) / denom)
    solved = [values[layers - 1]]
    for layer in range(layers - 2, -1, -1):
        solved.insert(0, values[layer] - primes[layer] * solved[0])
    return jnp.stack(solved, axis=1)

def reference(velocity_start, forcing, rate_factor, basal_drag, edge_weight, nbr_local, send_list, ice_mask):
    highest = lax.Precision.HIGHEST
    iced = ice_mask.astype(jnp.float32)
    viscosity = viscosity_of(velocity_start, rate_factor)
    face_visc = 0.5 * (viscosity[:-1] + viscosity[1:])
    weight_total = lax.optimization_barrier(jnp.sum(edge_weight, axis=0))

    def apply_op(field):
        near = neighbours(iced * viscosity * field, send_list, nbr_local, edge_weight)
        inner = local_terms(field, viscosity, face_visc, weight_total, basal_drag)
        return iced * (inner - near) + (1.0 - iced) * field
    lower, middle, upper = band_terms(viscosity, face_visc, weight_total, basal_drag, iced)
    mean_visc = lax.optimization_barrier(jnp.mean(viscosity, axis=0))
    coarse_diag = iced * (basal_drag / L + (weight_total + 1.0) * mean_visc) + (1.0 - iced)

    def coarse_op(field):
        near = neighbours(iced * mean_visc * field, send_list, nbr_local, edge_weight)
        inner = (weight_total + 1.0) * mean_visc * field + basal_drag * field / L
        return iced * (inner - near) + (1.0 - iced) * field

    def precondition(right):
        smooth = thomas(lower, middle, upper, right)
        restricted = lax.optimization_barrier(jnp.mean(right - apply_op(smooth), axis=1))
        correction = 0.8 * restricted / coarse_diag
        for sweep in range(SWEEPS - 1):
            correction = correction + 0.8 * (restricted - coarse_op(correction)) / coarse_diag
        return smooth + correction[:, None, :]
    newton_residual = apply_op(velocity_start) - iced * forcing
    start_resid = -newton_residual
    beta_zero = jnp.sqrt(jnp.sum(start_resid * start_resid) + 1e-12)
    basis = [start_resid / beta_zero]
    directions = []
    hessen = jnp.zeros((M + 1, M), jnp.float32)
    for inner_step in range(M):
        direction = precondition(basis[inner_step])
        image = apply_op(direction)
        stacked = jnp.stack(basis)
        proj = jnp.einsum('jabc,abc->j', stacked, image, precision=highest)
        image = image - jnp.einsum('j,jabc->abc', proj, stacked, precision=highest)
        length = jnp.sqrt(jnp.sum(image * image) + 1e-12)
        hessen = hessen.at[:inner_step + 1, inner_step].set(proj)
        hessen = hessen.at[inner_step + 1, inner_step].set(length)
        basis.append(image / length)
        directions.append(direction)
    gram = jnp.dot(hessen.T, hessen, precision=highest)
    factor = jnp.linalg.cholesky(gram)
    coeffs = jax.scipy.linalg.cho_solve((factor, True), beta_zero * hessen[0])
    update = jnp.einsum('j,jabc->abc', coeffs, jnp.stack(directions), precision=highest)
    return (velocity_start + update, newton_residual)
```

```python
import functools

import jax
import jax.numpy as jnp
from jax import lax
from jax.experimental import pallas as pl
from jax.experimental.pallas import tpu as pltpu
from jax.sharding import PartitionSpec as P

M = 4
NB = 6
REACH = 32
LANES = 128
MESH = pl.DeviceIdType.MESH


def pick(value, index):
    return jnp.take_along_axis(value, index, axis=1, mode="promise_in_bounds")


def kernel(
    n, layers,
    vel, frc, rate, drag, ew, nbr, send, mask, vel_out, res_out,
    v2, f2, iv2, inv2, li2, pr2, td2, x2, h2, ivh2, w2, s2, u2, z2, ewf, idxf, ewc, nbc, tab,
    msg, got, smsg, sgot, imsg, igot, red,
    hs, hr, ss, sr, is_, ir, rs, rr,
):
    me = lax.axis_index("region")
    barrier = pltpu.get_barrier_semaphore()
    for off in range(1, n):
        pl.semaphore_signal(
            barrier, inc=1, device_id={"region": lax.rem(me + off, n)}, device_id_type=MESH
        )
    has_low, has_up = me > 0, me < n - 1
    sub = lax.broadcasted_iota(jnp.int32, (8, LANES), 0)
    lane = lax.broadcasted_iota(jnp.int32, (8, LANES), 1)
    tile = sub & 3
    width = 4 * LANES
    tail = lane >= LANES - REACH
    zero = jnp.zeros((8, LANES), jnp.float32)

    def row(ref, layer):
        return ref[pl.ds(8 * layer, 8), :]

    def put(ref, layer, value):
        ref[pl.ds(8 * layer, 8), :] = value

    def spread(ref, first, count, value):
        ref[pl.ds(first, count, stride=8), :] = value

    def gathered(ref, first, count):
        return ref[pl.ds(first, count, stride=8), :]

    for side, at, line in ((0, 0, 0), (1, 3, 1)):
        imsg[side, 0:NB, :] = nbr[:, at * LANES:(at + 1) * LANES]
        imsg[side, NB:8, :] = jnp.zeros((2, LANES), jnp.int32)
        imsg[side, NB:NB + 1, 0:REACH] = send[line:line + 1, :]

    for c in range(2):
        for t in range(4):
            cols = slice(t * LANES, (t + 1) * LANES)
            spread(v2, 4 * c + t, layers, vel[c, :, cols])
            spread(f2, 4 * c + t, layers, frc[c, :, cols])
            spread(iv2, 4 * c + t, layers, rate[:, cols])
            spread(ewf, 4 * c + t, NB, ew[:, cols])
    for k in range(NB):
        put(ewc, k, zero)
        put(nbc, k, jnp.zeros((8, LANES), jnp.int32))
    for t in range(4):
        cols = slice(t * LANES, (t + 1) * LANES)
        spread(ewc, 1 + t, NB, ew[:, cols])
        spread(nbc, 1 + t, NB, nbr[:, cols])
    ice4 = mask[...].astype(jnp.float32)
    iced = jnp.concatenate([ice4, ice4], axis=0)
    drag4 = drag[...]
    bed = jnp.concatenate([drag4, drag4], axis=0)
    h2[...] = jnp.zeros_like(h2)
    ivh2[...] = jnp.zeros_like(ivh2)

    total = row(ewf, 0)
    for k in range(1, NB):
        total = total + row(ewf, k)
    here = row(v2, 0)
    mean = zero
    for l in range(layers):
        if l < layers - 1:
            above = row(v2, l + 1)
            step = above - here
            square = step * step
            shear = square + pltpu.roll(square, 4, 0)
            here = above
            visc = row(iv2, l) * jnp.exp(jnp.log(1.0 + shear) * (-1.0 / 3.0))
        else:
            visc = row(iv2, l)
        mean = mean + visc
        put(iv2, l, visc)
    mean = mean * (1.0 / layers)
    factor = iced * (total + 1.0)
    other = 1.0 - iced
    coarse_diag = factor * mean + iced * (bed * (1.0 / layers)) + other
    put(s2, 0, 0.8 * iced / coarse_diag)
    put(s2, 1, iced * mean)
    below = zero
    last = zero
    prior = zero
    for l in range(layers):
        visc = row(iv2, l)
        diag = factor * visc + other
        if l == 0:
            diag = diag + iced * bed
        put(td2, l, diag)
        if l < layers - 1:
            face = iced * (2.0 * (visc + row(iv2, l + 1)))
        else:
            face = zero
        inverse = 1.0 / (diag + face + below - below * prior)
        put(inv2, l, inverse)
        put(li2, l, below * inverse)
        prior = face * inverse
        put(pr2, l, prior)
        value = row(v2, l)
        image = diag * value - iced * row(f2, l)
        if l < layers - 1:
            flux = face * (row(v2, l + 1) - value)
            image = image - flux
        else:
            flux = zero
        put(w2, l, image + last)
        last = flux
        below = face
    for l in range(layers):
        scaled = iced * row(iv2, l)
        put(iv2, l, scaled)
        put(x2, l, scaled * row(v2, l))
    for side, s in ((0, 0), (1, 3)):
        smsg[side, 0:layers, :] = gathered(x2, s, layers)
        smsg[side, 24:24 + layers, :] = gathered(x2, s + 4, layers)
        smsg[side, 48:48 + layers, :] = gathered(iv2, s, layers)
        smsg[side, 72:74, :] = gathered(s2, s, 2)
        smsg[side, 74:80, :] = ew[:, s * LANES:(s + 1) * LANES]

    def exchange(parts):
        low, up = me - 1, me + 1

        def copies(side):
            peer = low if side == 0 else up
            return [
                pltpu.make_async_remote_copy(
                    src_ref=src.at[side], dst_ref=dst.at[1 - side],
                    send_sem=ssem.at[side], recv_sem=rsem.at[1 - side],
                    device_id={"region": peer}, device_id_type=MESH,
                )
                for src, dst, ssem, rsem in parts
            ]

        def arrivals(side):
            peer = low if side == 0 else up
            return [
                pltpu.make_async_remote_copy(
                    src_ref=src.at[1 - side], dst_ref=dst.at[side],
                    send_sem=ssem.at[1 - side], recv_sem=rsem.at[side],
                    device_id={"region": peer}, device_id_type=MESH,
                )
                for src, dst, ssem, rsem in parts
            ]

        @pl.when(has_low)
        def _():
            for copy in copies(0):
                copy.start()

        @pl.when(has_up)
        def _():
            for copy in copies(1):
                copy.start()

        def finish(unpack):
            for side, there in ((0, has_low), (1, has_up)):
                @pl.when(there)
                def _():
                    for copy in arrivals(side):
                        copy.wait_recv()
                    unpack(side)

            for side, there in ((0, has_low), (1, has_up)):
                @pl.when(there)
                def _():
                    for copy in copies(side):
                        copy.wait_send()

        return finish

    pl.semaphore_wait(barrier, n - 1)
    finish = exchange([(imsg, igot, is_, ir), (smsg, sgot, ss, sr)])
    put(tab, 0, jnp.full((8, LANES), width - REACH, jnp.int32))
    put(tab, 1, jnp.zeros((8, LANES), jnp.int32))

    tab[5:6, :] = imsg[1, NB:NB + 1, :]
    tab[8:9, :] = imsg[0, NB:NB + 1, :]
    h3 = s2.at[pl.ds(16, 16)]
    h3[...] = jnp.zeros((16, LANES), jnp.float32)

    def unpack_first(side):
        s = 0 if side == 0 else 3
        place = 0 if side == 0 else 5
        spread(h2, s, layers, sgot[side, 0:layers, :])
        spread(h2, s + 4, layers, sgot[side, 24:24 + layers, :])
        spread(ivh2, s, layers, sgot[side, 48:48 + layers, :])
        spread(ivh2, s + 4, layers, sgot[side, 48:48 + layers, :])
        spread(h3, place, 2, sgot[side, 72:74, :])
        spread(ewc, place, NB, sgot[side, 74:80, :])
        spread(nbc, place, NB, igot[side, 0:NB, :])
        if side == 0:
            tab[1:2, :] = igot[0, NB:NB + 1, :]
        else:
            tab[12:13, :] = igot[1, NB:NB + 1, :]

    finish(unpack_first)

    middle_rows = (sub >= 1) & (sub <= 4)
    coarse_a = jnp.where(middle_rows, pltpu.roll(row(s2, 0), 1, 0), row(s2, 2))
    coarse_b = jnp.where(middle_rows, pltpu.roll(row(s2, 1), 1, 0), row(s2, 3))
    base = jnp.where(sub == 0, 3 * LANES, jnp.where(sub == 5, 0, (sub - 1) * LANES))
    index_c, high_c, weight_c = [], [], []
    for k in range(NB):
        p = row(nbc, k)
        low_col = pick(row(tab, 0), p & (LANES - 1)) - width
        up_col = pick(row(tab, 1), (p - (width + REACH)) & (LANES - 1)) + width
        col = jnp.where(p < REACH, low_col, jnp.where(p >= width + REACH, up_col, p - REACH))
        rel = col - base
        index_c.append(rel & (LANES - 1))
        high_c.append(rel >= LANES - REACH)
        weight_c.append(row(ewc, k))
        fine = jnp.where(sub < 4, pltpu.roll(rel, 7, 0), pltpu.roll(rel, 3, 0))
        put(idxf, k, fine)
        put(ewf, k, iced * row(ewf, k))

    def near(value, before, after, index, high, weight):
        first = jnp.where(tail, before, value)
        second = jnp.where(tail, value, after)
        acc = None
        for k in range(NB):
            got_k = jnp.where(high[k], pick(second, index[k]), pick(first, index[k]))
            term = weight[k] * got_k
            acc = term if acc is None else acc + term
        return acc

    def near_coarse(value):
        return near(
            value, pltpu.roll(value, 1, 0), pltpu.roll(value, 7, 0), index_c, high_c, weight_c
        )

    first_tile, last_tile = tile == 0, tile == 3

    def near_fine(value, halo):
        before = jnp.where(first_tile, halo, pltpu.roll(value, 1, 0))
        after = jnp.where(last_tile, halo, pltpu.roll(value, 7, 0))
        index, high, weight = [], [], []
        for k in range(NB):
            rel = row(idxf, k)
            index.append(rel & (LANES - 1))
            high.append(rel >= LANES - REACH)
            weight.append(row(ewf, k))
        return near(value, before, after, index, high, weight)

    def first_residual(l, norm):
        at = pl.ds(pl.multiple_of(8 * l, 8), 8)
        resid = w2[at, :] - near_fine(x2[at, :], h2[at, :])
        w2[at, :] = resid
        u2[0, at, :] = -resid
        return norm + resid * resid

    norm = lax.fori_loop(0, layers, first_residual, zero, unroll=True)
    for c in range(2):
        for t in range(4):
            res_out[c, :, t * LANES:(t + 1) * LANES] = gathered(w2, 4 * c + t, layers)

    def flat(value):
        return jnp.sum(value, axis=0, keepdims=True)

    def reduce_all(step, values):
        mine = red.at[step, me]
        mine[...] = jnp.concatenate(
            [flat(v) for v in values] + [jnp.zeros((8 - len(values), LANES), jnp.float32)], axis=0
        )

        def copy(peer, slot):
            return pltpu.make_async_remote_copy(
                src_ref=red.at[step, me], dst_ref=red.at[step, slot],
                send_sem=rs.at[step, peer], recv_sem=rr.at[step, slot],
                device_id={"region": peer}, device_id_type=MESH,
            )

        for off in range(1, n):
            copy(lax.rem(me + off, n), me).start()

        def finish():
            for off in range(1, n):
                peer = lax.rem(me + n - off, n)
                copy(peer, peer).wait_recv()
            total = red[step, 0]
            for slot in range(1, n):
                total = total + red[step, slot]
            for off in range(1, n):
                copy(lax.rem(me + off, n), me).wait_send()
            full = jnp.sum(total, axis=1, keepdims=True)
            return [full[i:i + 1, :] for i in range(len(values))]

        return finish

    sizes, hess, grams = [], [], []
    for j in range(M):
        uj, zj = u2.at[j], z2.at[j]
        values = [row(uj, 0) * row(inv2, 0)]
        for l in range(1, layers):
            values.append(row(uj, l) * row(inv2, l) + row(li2, l) * values[l - 1])
        solved = values[layers - 1]
        mean = zero
        for l in range(layers - 1, -1, -1):
            if l < layers - 1:
                solved = values[l] + row(pr2, l) * solved
            put(zj, l, solved)
            weighted = row(iv2, l) * solved
            put(x2, l, weighted)
            mean = mean + weighted
        put(x2, layers, mean * (1.0 / layers))
        for side, s in ((0, 0), (1, 3)):
            msg[j, side, 0:layers + 1, :] = gathered(x2, s, layers + 1)
            msg[j, side, 24:25 + layers, :] = gathered(x2, s + 4, layers + 1)
        finish = exchange([(msg.at[j], got.at[j], hs.at[j], hr.at[j])])

        def unpack(side, j=j):
            s = 0 if side == 0 else 3
            spread(h2, s, layers + 1, got[j, side, 0:layers + 1, :])
            spread(h2, s + 4, layers + 1, got[j, side, 24:25 + layers, :])

        finish(unpack)
        own, halo = row(x2, layers), row(h2, layers)
        outer = [
            jnp.where(sub == 0, halo, jnp.where(sub == 5, pltpu.roll(halo, 2, 0), 0.0)),
            jnp.where(
                sub == 0, pltpu.roll(halo, 4, 0), jnp.where(sub == 5, pltpu.roll(halo, 6, 0), 0.0)
            ),
        ]
        result = []
        for c in range(2):
            start = jnp.where(middle_rows, pltpu.roll(own, 1 if c == 0 else 5, 0), outer[c])
            source = near_coarse(start)
            corr = coarse_a * source
            for sweep in range(2):
                corr = 0.2 * corr + coarse_a * (source + near_coarse(coarse_b * corr))
            result.append(corr)
        e0, e1 = result
        corr = jnp.where(sub < 4, pltpu.roll(e0, 7, 0), pltpu.roll(e1, 3, 0))
        corr_halo = jnp.where(
            sub < 4,
            jnp.where(sub == 0, e0, pltpu.roll(e0, 6, 0)),
            jnp.where(sub == 4, pltpu.roll(e1, 4, 0), pltpu.roll(e1, 2, 0)),
        )

        def image(l, carry, j=j, uj=uj, zj=zj, corr=corr, corr_halo=corr_halo):
            at = pl.ds(pl.multiple_of(8 * l, 8), 8)
            zj[at, :] = zj[at, :] + corr
            value = x2[at, :] + iv2[at, :] * corr
            halo = h2[at, :] + ivh2[at, :] * corr_halo
            w = uj[at, :] + td2[at, :] * corr - near_fine(value, halo)
            w2[at, :] = w
            out = [carry[i] + u2[i, at, :] * w for i in range(j + 1)]
            if j == M - 1:
                out.append(carry[j + 1] + w * w)
            return tuple(out)

        count = j + 1 + (j == M - 1)
        dots = lax.fori_loop(0, layers, image, (zero,) * count, unroll=True)
        reduced = reduce_all(j, list(dots) + [norm])()
        size = jnp.sqrt(reduced[-1] + 1e-12)
        sizes.append(size)
        column = [reduced[i] / sizes[i] / size for i in range(j + 1)]
        hess.append(column)
        if j < M - 1:
            inverse = 1.0 / size
            scale = [column[i] / sizes[i] for i in range(j + 1)]
            inverse = jnp.broadcast_to(inverse, (8, LANES))
            scale = [jnp.broadcast_to(s, (8, LANES)) for s in scale]

            def next_basis(l, norm, j=j, scale=scale, inverse=inverse):
                at = pl.ds(pl.multiple_of(8 * l, 8), 8)
                fresh = w2[at, :] * inverse
                for i in range(j + 1):
                    fresh = fresh - scale[i] * u2[i, at, :]
                u2[j + 1, at, :] = fresh
                return norm + fresh * fresh

            norm = lax.fori_loop(0, layers, next_basis, zero, unroll=True)
        else:
            square = reduced[M] / size / size
            for i in range(M):
                square = square - column[i] * column[i]
            last_square = jnp.maximum(square, 0.0) + 1e-12

    def entry(i, j):
        if i <= j:
            return hess[j][i]
        return sizes[i] if i == j + 1 else None

    gram = [[None] * M for _ in range(M)]
    for a in range(M):
        for b in range(a + 1):
            acc = None
            for i in range(min(a, b) + 2):
                if i == M:
                    term = last_square
                else:
                    left, right = entry(i, a), entry(i, b)
                    if left is None or right is None:
                        continue
                    term = left * right
                acc = term if acc is None else acc + term
            gram[a][b] = acc
    right = [sizes[0] * hess[j][0] for j in range(M)]
    chol = [[None] * M for _ in range(M)]
    inv_diag = []
    for a in range(M):
        for b in range(a + 1):
            acc = gram[a][b]
            for i in range(b):
                acc = acc - chol[a][i] * chol[b][i]
            if a == b:
                root = jnp.sqrt(acc)
                inv_diag.append(1.0 / root)
            else:
                chol[a][b] = acc * inv_diag[b]
    forward = []
    for a in range(M):
        acc = right[a]
        for i in range(a):
            acc = acc - chol[a][i] * forward[i]
        forward.append(acc * inv_diag[a])
    coeffs = [None] * M
    for a in range(M - 1, -1, -1):
        acc = forward[a]
        for i in range(a + 1, M):
            acc = acc - chol[i][a] * coeffs[i]
        coeffs[a] = acc * inv_diag[a]
    coeffs = [jnp.broadcast_to(coeffs[j] / sizes[j], (8, LANES)) for j in range(M)]
    for l in range(layers):
        value = row(v2, l)
        for j in range(M):
            value = value + coeffs[j] * row(z2.at[j], l)
        put(w2, l, value)
    for c in range(2):
        for t in range(4):
            vel_out[c, :, t * LANES:(t + 1) * LANES] = gathered(w2, 4 * c + t, layers)


def body(velocity_start, forcing, rate_factor, basal_drag, edge_weight, nbr_local, send_list, ice_mask):
    n = lax.axis_size("region")
    layers = velocity_start.shape[1]
    full = 8 * layers
    f32, i32 = jnp.float32, jnp.int32
    V, D = pltpu.VMEM, pltpu.SemaphoreType.DMA
    spec = pl.BlockSpec(memory_space=pltpu.VMEM)
    shape = jax.ShapeDtypeStruct(velocity_start.shape, f32)
    field = V((full, LANES), f32)
    return tuple(pl.pallas_call(
        functools.partial(kernel, n, layers),
        out_shape=(shape, shape),
        in_specs=[spec] * 8,
        out_specs=(spec, spec),
        scratch_shapes=[
            field, field, field, field, field, field, field,
            V((full + 8, LANES), f32), V((full + 8, LANES), f32), field, field, V((32, LANES), f32),
            V((M, full, LANES), f32), V((M, full, LANES), f32),
            V((8 * NB, LANES), f32), V((8 * NB, LANES), i32),
            V((8 * NB, LANES), f32), V((8 * NB, LANES), i32), V((16, LANES), i32),
            V((M, 2, 48, LANES), f32), V((M, 2, 48, LANES), f32),
            V((2, 80, LANES), f32), V((2, 80, LANES), f32),
            V((2, 8, LANES), i32), V((2, 8, LANES), i32),
            V((M, n, 8, LANES), f32),
            D((M, 2)), D((M, 2)), D((2,)), D((2,)), D((2,)), D((2,)), D((M, n)), D((M, n)),
        ],
        compiler_params=pltpu.CompilerParams(
            collective_id=0, has_side_effects=True, vmem_limit_bytes=32 * 1024 * 1024
        ),
    )(
        velocity_start, forcing, rate_factor, basal_drag.reshape(4, LANES), edge_weight, nbr_local,
        send_list, ice_mask.reshape(4, LANES),
    ))


def solution(mesh):
    cols = P(None, None, ("ens", "region"))
    in_specs = (
        cols, cols, P(None, ("ens", "region")), P("region"), P(None, "region"), P(None, "region"),
        P(None, "region"), P("region"),
    )
    return jax.shard_map(body, mesh=mesh, in_specs=in_specs, out_specs=(cols, cols), check_vma=False)
```

```python
import functools

import jax
import jax.numpy as jnp
from jax import lax
from jax.experimental import pallas as pl
from jax.experimental.pallas import tpu as pltpu
from jax.sharding import PartitionSpec as P

M = 4
NB = 6
REACH = 32
LANES = 128
MESH = pl.DeviceIdType.MESH


def pick(value, index):
    return jnp.take_along_axis(value, index, axis=1, mode="promise_in_bounds")


def kernel(
    n, inner, layers,
    vel, frc, rate, drag, ew, nbr, send, mask, vel_out, res_out,
    v2, f2, iv2, inv2, li2, pr2, td2, x2, h2, ivh2, w2, s2, u2, z2, q2, g2, ewf, idxf, ewc, nbc, tab,
    msg, got, smsg, sgot, imsg, igot, red0, red1,
    hs, hr, ss, sr, is_, ir, rs0, rr0, rs1, rr1,
):
    me = lax.axis_index("region")
    barrier = pltpu.get_barrier_semaphore()
    for off in range(1, n):
        pl.semaphore_signal(
            barrier, inc=1, device_id={"region": lax.rem(me + off, n)}, device_id_type=MESH
        )
    has_low, has_up = me > 0, me < n - 1
    sub = lax.broadcasted_iota(jnp.int32, (8, LANES), 0)
    lane = lax.broadcasted_iota(jnp.int32, (8, LANES), 1)
    tile = sub & 3
    width = 4 * LANES
    tail = lane >= LANES - REACH
    zero = jnp.zeros((8, LANES), jnp.float32)

    def row(ref, layer):
        return ref[pl.ds(8 * layer, 8), :]

    def put(ref, layer, value):
        ref[pl.ds(8 * layer, 8), :] = value

    def spread(ref, first, count, value):
        ref[pl.ds(first, count, stride=8), :] = value

    def gathered(ref, first, count):
        return ref[pl.ds(first, count, stride=8), :]

    for side, at, line in ((0, 0, 0), (1, 3, 1)):
        imsg[side, 0:NB, :] = nbr[:, at * LANES:(at + 1) * LANES]
        imsg[side, NB:8, :] = jnp.zeros((2, LANES), jnp.int32)
        imsg[side, NB:NB + 1, 0:REACH] = send[line:line + 1, :]

    for c in range(2):
        for t in range(4):
            cols = slice(t * LANES, (t + 1) * LANES)
            spread(v2, 4 * c + t, layers, vel[c, :, cols])
            spread(f2, 4 * c + t, layers, frc[c, :, cols])
            spread(iv2, 4 * c + t, layers, rate[:, cols])
            spread(ewf, 4 * c + t, NB, ew[:, cols])
    for k in range(NB):
        put(ewc, k, zero)
        put(nbc, k, jnp.zeros((8, LANES), jnp.int32))
    for t in range(4):
        cols = slice(t * LANES, (t + 1) * LANES)
        spread(ewc, 1 + t, NB, ew[:, cols])
        spread(nbc, 1 + t, NB, nbr[:, cols])
    ice4 = mask[...].astype(jnp.float32)
    iced = jnp.concatenate([ice4, ice4], axis=0)
    drag4 = drag[...]
    bed = jnp.concatenate([drag4, drag4], axis=0)
    h2[...] = jnp.zeros_like(h2)
    ivh2[...] = jnp.zeros_like(ivh2)

    total = row(ewf, 0)
    for k in range(1, NB):
        total = total + row(ewf, k)
    here = row(v2, 0)
    mean = zero
    for l in range(layers):
        if l < layers - 1:
            above = row(v2, l + 1)
            step = above - here
            square = step * step
            shear = square + pltpu.roll(square, 4, 0)
            here = above
            visc = row(iv2, l) * jnp.exp(jnp.log(1.0 + shear) * (-1.0 / 3.0))
        else:
            visc = row(iv2, l)
        mean = mean + visc
        put(iv2, l, visc)
    mean = mean * (1.0 / layers)
    factor = iced * (total + 1.0)
    other = 1.0 - iced
    coarse_diag = factor * mean + iced * (bed * (1.0 / layers)) + other
    put(s2, 0, 0.8 * iced / coarse_diag)
    put(s2, 1, iced * mean)
    below = zero
    last = zero
    prior = zero
    for l in range(layers):
        visc = row(iv2, l)
        diag = factor * visc + other
        if l == 0:
            diag = diag + iced * bed
        put(td2, l, diag)
        if l < layers - 1:
            face = iced * (2.0 * (visc + row(iv2, l + 1)))
        else:
            face = zero
        inverse = 1.0 / (diag + face + below - below * prior)
        put(inv2, l, inverse)
        put(li2, l, below * inverse)
        prior = face * inverse
        put(pr2, l, prior)
        value = row(v2, l)
        image = diag * value - iced * row(f2, l)
        if l < layers - 1:
            flux = face * (row(v2, l + 1) - value)
            image = image - flux
        else:
            flux = zero
        put(w2, l, image + last)
        last = flux
        below = face
    for l in range(layers):
        scaled = iced * row(iv2, l)
        put(iv2, l, scaled)
        put(x2, l, scaled * row(v2, l))
    for side, s in ((0, 0), (1, 3)):
        smsg[side, 0:layers, :] = gathered(x2, s, layers)
        smsg[side, 24:24 + layers, :] = gathered(x2, s + 4, layers)
        smsg[side, 48:48 + layers, :] = gathered(iv2, s, layers)
        smsg[side, 72:74, :] = gathered(s2, s, 2)
        smsg[side, 74:80, :] = ew[:, s * LANES:(s + 1) * LANES]

    def exchange(parts):
        low, up = me - 1, me + 1

        def copies(side):
            peer = low if side == 0 else up
            return [
                pltpu.make_async_remote_copy(
                    src_ref=src.at[side], dst_ref=dst.at[1 - side],
                    send_sem=ssem.at[side], recv_sem=rsem.at[1 - side],
                    device_id={"region": peer}, device_id_type=MESH,
                )
                for src, dst, ssem, rsem in parts
            ]

        def arrivals(side):
            peer = low if side == 0 else up
            return [
                pltpu.make_async_remote_copy(
                    src_ref=src.at[1 - side], dst_ref=dst.at[side],
                    send_sem=ssem.at[1 - side], recv_sem=rsem.at[side],
                    device_id={"region": peer}, device_id_type=MESH,
                )
                for src, dst, ssem, rsem in parts
            ]

        @pl.when(has_low)
        def _():
            for copy in copies(0):
                copy.start()

        @pl.when(has_up)
        def _():
            for copy in copies(1):
                copy.start()

        def finish(unpack):
            for side, there in ((0, has_low), (1, has_up)):
                @pl.when(there)
                def _():
                    for copy in arrivals(side):
                        copy.wait_recv()
                    unpack(side)

            for side, there in ((0, has_low), (1, has_up)):
                @pl.when(there)
                def _():
                    for copy in copies(side):
                        copy.wait_send()

        return finish

    pl.semaphore_wait(barrier, n - 1)
    finish = exchange([(imsg, igot, is_, ir), (smsg, sgot, ss, sr)])
    put(tab, 0, jnp.full((8, LANES), width - REACH, jnp.int32))
    put(tab, 1, jnp.zeros((8, LANES), jnp.int32))

    tab[5:6, :] = imsg[1, NB:NB + 1, :]
    tab[8:9, :] = imsg[0, NB:NB + 1, :]
    h3 = s2.at[pl.ds(16, 16)]
    h3[...] = jnp.zeros((16, LANES), jnp.float32)

    def unpack_first(side):
        s = 0 if side == 0 else 3
        place = 0 if side == 0 else 5
        spread(h2, s, layers, sgot[side, 0:layers, :])
        spread(h2, s + 4, layers, sgot[side, 24:24 + layers, :])
        spread(ivh2, s, layers, sgot[side, 48:48 + layers, :])
        spread(ivh2, s + 4, layers, sgot[side, 48:48 + layers, :])
        spread(h3, place, 2, sgot[side, 72:74, :])
        spread(ewc, place, NB, sgot[side, 74:80, :])
        spread(nbc, place, NB, igot[side, 0:NB, :])
        if side == 0:
            tab[1:2, :] = igot[0, NB:NB + 1, :]
        else:
            tab[12:13, :] = igot[1, NB:NB + 1, :]

    finish(unpack_first)

    middle_rows = (sub >= 1) & (sub <= 4)
    coarse_a = jnp.where(middle_rows, pltpu.roll(row(s2, 0), 1, 0), row(s2, 2))
    coarse_b = jnp.where(middle_rows, pltpu.roll(row(s2, 1), 1, 0), row(s2, 3))
    base = jnp.where(sub == 0, 3 * LANES, jnp.where(sub == 5, 0, (sub - 1) * LANES))
    index_c, high_c, weight_c = [], [], []
    for k in range(NB):
        p = row(nbc, k)
        low_col = pick(row(tab, 0), p & (LANES - 1)) - width
        up_col = pick(row(tab, 1), (p - (width + REACH)) & (LANES - 1)) + width
        col = jnp.where(p < REACH, low_col, jnp.where(p >= width + REACH, up_col, p - REACH))
        rel = col - base
        index_c.append(rel & (LANES - 1))
        high_c.append(rel >= LANES - REACH)
        weight_c.append(row(ewc, k))
        fine = jnp.where(sub < 4, pltpu.roll(rel, 7, 0), pltpu.roll(rel, 3, 0))
        put(idxf, k, fine)
        put(ewf, k, iced * row(ewf, k))

    def near(value, before, after, index, high, weight):
        first = jnp.where(tail, before, value)
        second = jnp.where(tail, value, after)
        acc = None
        for k in range(NB):
            got_k = jnp.where(high[k], pick(second, index[k]), pick(first, index[k]))
            term = weight[k] * got_k
            acc = term if acc is None else acc + term
        return acc

    def near_coarse(value):
        return near(
            value, pltpu.roll(value, 1, 0), pltpu.roll(value, 7, 0), index_c, high_c, weight_c
        )

    first_tile, last_tile = tile == 0, tile == 3

    def near_fine(value, halo):
        before = jnp.where(first_tile, halo, pltpu.roll(value, 1, 0))
        after = jnp.where(last_tile, halo, pltpu.roll(value, 7, 0))
        index, high, weight = [], [], []
        for k in range(NB):
            rel = row(idxf, k)
            index.append(rel & (LANES - 1))
            high.append(rel >= LANES - REACH)
            weight.append(row(ewf, k))
        return near(value, before, after, index, high, weight)

    def first_residual(l, norm):
        at = pl.ds(pl.multiple_of(8 * l, 8), 8)
        resid = w2[at, :] - near_fine(x2[at, :], h2[at, :])
        w2[at, :] = resid
        u2[0, at, :] = -resid
        return norm + resid * resid

    norm = lax.fori_loop(0, layers, first_residual, zero, unroll=True)
    for c in range(2):
        for t in range(4):
            res_out[c, :, t * LANES:(t + 1) * LANES] = gathered(w2, 4 * c + t, layers)

    def flat(value):
        return jnp.sum(value, axis=0, keepdims=True)

    ia, ib = lax.rem(me, inner), lax.div(me, inner)

    def partner(phase, off):
        if phase == 0:
            spot = lax.rem(ia + off, inner)
            return spot, ib * inner + spot
        spot = lax.rem(ib + off, n // inner)
        return spot, spot * inner + ia

    reds = ((red0, rs0, rr0, inner, ia), (red1, rs1, rr1, n // inner, ib))

    def phase_start(phase, step, tile_value):
        red, rs, rr, group, mine = reds[phase]
        red[step, mine] = tile_value
        for off in range(1, group):
            spot, peer = partner(phase, off)
            pltpu.make_async_remote_copy(
                src_ref=red.at[step, mine], dst_ref=red.at[step, mine],
                send_sem=rs.at[step, spot], recv_sem=rr.at[step, mine],
                device_id={"region": peer}, device_id_type=MESH,
            ).start()

    def phase_end(phase, step):
        red, rs, rr, group, mine = reds[phase]
        copies = []
        for off in range(1, group):
            spot, peer = partner(phase, off)
            copies.append(pltpu.make_async_remote_copy(
                src_ref=red.at[step, mine], dst_ref=red.at[step, spot],
                send_sem=rs.at[step, spot], recv_sem=rr.at[step, spot],
                device_id={"region": peer}, device_id_type=MESH,
            ))
        for copy in copies:
            copy.wait_recv()
        total = red[step, 0]
        for slot in range(1, group):
            total = total + red[step, slot]
        for copy in copies:
            copy.wait_send()
        return total

    def reduce_start(step, values):
        blank = jnp.zeros((8 - len(values), LANES), jnp.float32)
        phase_start(0, step, jnp.concatenate([flat(v) for v in values] + [blank], axis=0))

    def reduce_middle(step):
        phase_start(1, step, phase_end(0, step))

    def reduce_end(step):
        full = jnp.sum(phase_end(1, step), axis=1, keepdims=True)
        return [full[i:i + 1, :] for i in range(8)]

    def wide(value):
        return jnp.broadcast_to(value, (8, LANES))

    def layer_rows(l):
        return pl.ds(pl.multiple_of(8 * l, 8), 8)

    def mix(ref, j, scale, shifts, at):
        out = scale * ref[j, at, :]
        for i in range(j):
            out = out + shifts[i] * ref[i, at, :]
        return out

    def settle(j):
        sums = reduce_end(j)
        size = jnp.sqrt(sums[j + 1] + 1e-12)
        sizes.append(size)
        hess.append([sums[i] / sizes[i] / size for i in range(j + 1)])
        return sums

    def mix_directions(j):
        scale, shifts = mixes[j]

        def one(l, carry):
            at = layer_rows(l)
            z2[j, at, :] = mix(z2, j, scale, shifts, at)
            return carry

        lax.fori_loop(0, layers, one, 0, unroll=True)

    mixes = {}
    sizes, hess = [], []
    for j in range(M):
        uj, zj = (u2.at[0] if j == 0 else g2), z2.at[j]
        values = [row(uj, 0) * row(inv2, 0)]
        for l in range(1, layers):
            values.append(row(uj, l) * row(inv2, l) + row(li2, l) * values[l - 1])
        solved = values[layers - 1]
        mean = zero
        for l in range(layers - 1, -1, -1):
            if l < layers - 1:
                solved = values[l] + row(pr2, l) * solved
            put(zj, l, solved)
            weighted = row(iv2, l) * solved
            put(x2, l, weighted)
            mean = mean + weighted
        put(x2, layers, mean * (1.0 / layers))
        for side, s in ((0, 0), (1, 3)):
            msg[j, side, 0:layers + 1, :] = gathered(x2, s, layers + 1)
            msg[j, side, 24:25 + layers, :] = gathered(x2, s + 4, layers + 1)
        finish = exchange([(msg.at[j], got.at[j], hs.at[j], hr.at[j])])

        def unpack(side, j=j):
            s = 0 if side == 0 else 3
            spread(h2, s, layers + 1, got[j, side, 0:layers + 1, :])
            spread(h2, s + 4, layers + 1, got[j, side, 24:25 + layers, :])

        if j >= 2:
            mix_directions(j - 1)
        if j >= 1:
            reduce_middle(j - 1)
        finish(unpack)
        own, halo = row(x2, layers), row(h2, layers)
        outer = [
            jnp.where(sub == 0, halo, jnp.where(sub == 5, pltpu.roll(halo, 2, 0), 0.0)),
            jnp.where(
                sub == 0, pltpu.roll(halo, 4, 0), jnp.where(sub == 5, pltpu.roll(halo, 6, 0), 0.0)
            ),
        ]
        result = []
        for c in range(2):
            start = jnp.where(middle_rows, pltpu.roll(own, 1 if c == 0 else 5, 0), outer[c])
            source = near_coarse(start)
            corr = coarse_a * source
            for sweep in range(2):
                corr = 0.2 * corr + coarse_a * (source + near_coarse(coarse_b * corr))
            result.append(corr)
        e0, e1 = result
        corr = jnp.where(sub < 4, pltpu.roll(e0, 7, 0), pltpu.roll(e1, 3, 0))
        corr_halo = jnp.where(
            sub < 4,
            jnp.where(sub == 0, e0, pltpu.roll(e0, 6, 0)),
            jnp.where(sub == 4, pltpu.roll(e1, 4, 0), pltpu.roll(e1, 2, 0)),
        )

        def image(l, carry, j=j, uj=uj, zj=zj, corr=corr, corr_halo=corr_halo):
            at = layer_rows(l)
            zj[at, :] = zj[at, :] + corr
            value = x2[at, :] + iv2[at, :] * corr
            halo = h2[at, :] + ivh2[at, :] * corr_halo
            w = uj[at, :] + td2[at, :] * corr - near_fine(value, halo)
            q2[j, at, :] = w
            if j > 0:
                return carry
            g2[at, :] = w - uj[at, :]
            return (carry[0] + uj[at, :] * w,)

        dots = lax.fori_loop(0, layers, image, (zero,), unroll=True)
        if j == 0:
            dots = dots + (norm,)
        else:
            settle(j - 1)
            size, column = sizes[j - 1], hess[j - 1]
            shifts = [wide(-column[i] / sizes[i]) for i in range(j - 1)]
            shifts.append(wide((1.0 - column[j - 1]) / size))
            scale = wide(1.0 / size)
            mixes[j] = (scale, shifts)

            def orthogonal(l, carry, j=j, scale=scale, shifts=shifts):
                at = layer_rows(l)
                u = scale * g2[at, :]
                for i in range(j):
                    u = u + shifts[i] * u2[i, at, :]
                w = mix(q2, j, scale, shifts, at)
                if j < M - 1:
                    u2[j, at, :] = u
                    q2[j, at, :] = w
                    g2[at, :] = w - u
                out = [carry[i] + u2[i, at, :] * w for i in range(j)]
                out += [carry[j] + u * w, carry[j + 1] + u * u]
                if j == M - 1:
                    out.append(carry[j + 2] + w * w)
                return tuple(out)

            dots = lax.fori_loop(
                0, layers, orthogonal, (zero,) * (j + 2 + (j == M - 1)), unroll=True
            )
        reduce_start(j, list(dots))
    mix_directions(M - 1)
    reduce_middle(M - 1)
    square = settle(M - 1)[M + 1] / sizes[M - 1] / sizes[M - 1]
    for i in range(M):
        square = square - hess[M - 1][i] * hess[M - 1][i]
    last_square = jnp.maximum(square, 0.0) + 1e-12

    def entry(i, j):
        if i <= j:
            return hess[j][i]
        return sizes[i] if i == j + 1 else None

    gram = [[None] * M for _ in range(M)]
    for a in range(M):
        for b in range(a + 1):
            acc = None
            for i in range(min(a, b) + 2):
                if i == M:
                    term = last_square
                else:
                    left, right = entry(i, a), entry(i, b)
                    if left is None or right is None:
                        continue
                    term = left * right
                acc = term if acc is None else acc + term
            gram[a][b] = acc
    right = [sizes[0] * hess[j][0] for j in range(M)]
    chol = [[None] * M for _ in range(M)]
    inv_diag = []
    for a in range(M):
        for b in range(a + 1):
            acc = gram[a][b]
            for i in range(b):
                acc = acc - chol[a][i] * chol[b][i]
            if a == b:
                root = jnp.sqrt(acc)
                inv_diag.append(1.0 / root)
            else:
                chol[a][b] = acc * inv_diag[b]
    forward = []
    for a in range(M):
        acc = right[a]
        for i in range(a):
            acc = acc - chol[a][i] * forward[i]
        forward.append(acc * inv_diag[a])
    coeffs = [None] * M
    for a in range(M - 1, -1, -1):
        acc = forward[a]
        for i in range(a + 1, M):
            acc = acc - chol[i][a] * coeffs[i]
        coeffs[a] = acc * inv_diag[a]
    coeffs = [jnp.broadcast_to(coeffs[j] / sizes[j], (8, LANES)) for j in range(M)]
    for l in range(layers):
        value = row(v2, l)
        for j in range(M):
            value = value + coeffs[j] * row(z2.at[j], l)
        put(w2, l, value)
    for c in range(2):
        for t in range(4):
            vel_out[c, :, t * LANES:(t + 1) * LANES] = gathered(w2, 4 * c + t, layers)


def body(velocity_start, forcing, rate_factor, basal_drag, edge_weight, nbr_local, send_list, ice_mask):
    n = lax.axis_size("region")
    layers = velocity_start.shape[1]
    full = 8 * layers
    inner = max(g for g in range(1, n + 1) if n % g == 0 and g * g <= n)
    f32, i32 = jnp.float32, jnp.int32
    V, D = pltpu.VMEM, pltpu.SemaphoreType.DMA
    spec = pl.BlockSpec(memory_space=pltpu.VMEM)
    shape = jax.ShapeDtypeStruct(velocity_start.shape, f32)
    field = V((full, LANES), f32)
    return tuple(pl.pallas_call(
        functools.partial(kernel, n, inner, layers),
        out_shape=(shape, shape),
        in_specs=[spec] * 8,
        out_specs=(spec, spec),
        scratch_shapes=[
            field, field, field, field, field, field, field,
            V((full + 8, LANES), f32), V((full + 8, LANES), f32), field, field, V((32, LANES), f32),
            V((M, full, LANES), f32), V((M, full, LANES), f32), V((M, full, LANES), f32), field,
            V((8 * NB, LANES), f32), V((8 * NB, LANES), i32),
            V((8 * NB, LANES), f32), V((8 * NB, LANES), i32), V((16, LANES), i32),
            V((M, 2, 48, LANES), f32), V((M, 2, 48, LANES), f32),
            V((2, 80, LANES), f32), V((2, 80, LANES), f32),
            V((2, 8, LANES), i32), V((2, 8, LANES), i32),
            V((M, inner, 8, LANES), f32), V((M, n // inner, 8, LANES), f32),
            D((M, 2)), D((M, 2)), D((2,)), D((2,)), D((2,)), D((2,)), D((M, inner)), D((M, inner)),
            D((M, n // inner)), D((M, n // inner)),
        ],
        compiler_params=pltpu.CompilerParams(
            collective_id=0, has_side_effects=True, vmem_limit_bytes=32 * 1024 * 1024
        ),
    )(
        velocity_start, forcing, rate_factor, basal_drag.reshape(4, LANES), edge_weight, nbr_local,
        send_list, ice_mask.reshape(4, LANES),
    ))


def solution(mesh):
    cols = P(None, None, ("ens", "region"))
    in_specs = (
        cols, cols, P(None, ("ens", "region")), P("region"), P(None, "region"), P(None, "region"),
        P(None, "region"), P("region"),
    )
    return jax.shard_map(body, mesh=mesh, in_specs=in_specs, out_specs=(cols, cols), check_vma=False)
```

```python
import functools

import jax
import jax.numpy as jnp
from jax import lax
from jax.experimental import pallas as pl
from jax.experimental.pallas import tpu as pltpu
from jax.sharding import PartitionSpec as P

M = 4
NB = 6
REACH = 32
LANES = 128
MESH = pl.DeviceIdType.MESH


def pick(value, index):
    return jnp.take_along_axis(value, index, axis=1, mode="promise_in_bounds")


def kernel(
    n, inner, layers,
    vel, frc, rate, drag, ew, nbr, send, mask, vel_out, res_out,
    v2, f2, iv2, inv2, li2, pr2, td2, x2, h2, ivh2, w2, s2, u2, z2, ewf, idxf, ewc, nbc, tab,
    msg, got, smsg, sgot, imsg, igot, red0, red1,
    hs, hr, ss, sr, is_, ir, rs0, rr0, rs1, rr1,
):
    me = lax.axis_index("region")
    barrier = pltpu.get_barrier_semaphore()
    ia, ib = lax.rem(me, inner), lax.div(me, inner)
    has_low, has_up = me > 0, me < n - 1

    def partner(phase, off):
        if phase == 0:
            spot = lax.rem(ia + off, inner)
            return spot, ib * inner + spot
        spot = lax.rem(ib + off, n // inner)
        return spot, spot * inner + ia

    def greet(peer):
        pl.semaphore_signal(barrier, inc=1, device_id={"region": peer}, device_id_type=MESH)

    for phase, group in ((0, inner), (1, n // inner)):
        for off in range(1, group):
            greet(partner(phase, off)[1])
    far_low = has_low & (ia == 0)
    far_up = has_up & (ia == inner - 1)

    @pl.when(far_low)
    def _():
        greet(me - 1)

    @pl.when(far_up)
    def _():
        greet(me + 1)

    greeters = (inner - 1) + (n // inner - 1) + far_low.astype(jnp.int32) + far_up.astype(jnp.int32)
    sub = lax.broadcasted_iota(jnp.int32, (8, LANES), 0)
    lane = lax.broadcasted_iota(jnp.int32, (8, LANES), 1)
    tile = sub & 3
    width = 4 * LANES
    tail = lane >= LANES - REACH
    zero = jnp.zeros((8, LANES), jnp.float32)

    def row(ref, layer):
        return ref[pl.ds(8 * layer, 8), :]

    def put(ref, layer, value):
        ref[pl.ds(8 * layer, 8), :] = value

    def spread(ref, first, count, value):
        ref[pl.ds(first, count, stride=8), :] = value

    def gathered(ref, first, count):
        return ref[pl.ds(first, count, stride=8), :]

    for side, at, line in ((0, 0, 0), (1, 3, 1)):
        imsg[side, 0:NB, :] = nbr[:, at * LANES:(at + 1) * LANES]
        imsg[side, NB:8, :] = jnp.zeros((2, LANES), jnp.int32)
        imsg[side, NB:NB + 1, 0:REACH] = send[line:line + 1, :]

    for c in range(2):
        for t in range(4):
            cols = slice(t * LANES, (t + 1) * LANES)
            spread(v2, 4 * c + t, layers, vel[c, :, cols])
            spread(f2, 4 * c + t, layers, frc[c, :, cols])
            spread(iv2, 4 * c + t, layers, rate[:, cols])
            spread(ewf, 4 * c + t, NB, ew[:, cols])
    for k in range(NB):
        put(ewc, k, zero)
        put(nbc, k, jnp.zeros((8, LANES), jnp.int32))
    for t in range(4):
        cols = slice(t * LANES, (t + 1) * LANES)
        spread(ewc, 1 + t, NB, ew[:, cols])
        spread(nbc, 1 + t, NB, nbr[:, cols])
    ice4 = mask[...].astype(jnp.float32)
    iced = jnp.concatenate([ice4, ice4], axis=0)
    drag4 = drag[...]
    bed = jnp.concatenate([drag4, drag4], axis=0)
    h2[...] = jnp.zeros_like(h2)
    ivh2[...] = jnp.zeros_like(ivh2)

    total = row(ewf, 0)
    for k in range(1, NB):
        total = total + row(ewf, k)
    here = row(v2, 0)
    mean = zero
    for l in range(layers):
        if l < layers - 1:
            above = row(v2, l + 1)
            step = above - here
            square = step * step
            shear = square + pltpu.roll(square, 4, 0)
            here = above
            visc = row(iv2, l) * jnp.exp(jnp.log(1.0 + shear) * (-1.0 / 3.0))
        else:
            visc = row(iv2, l)
        mean = mean + visc
        put(iv2, l, visc)
    mean = mean * (1.0 / layers)
    factor = iced * (total + 1.0)
    other = 1.0 - iced
    coarse_diag = factor * mean + iced * (bed * (1.0 / layers)) + other
    put(s2, 0, 0.8 * iced / coarse_diag)
    put(s2, 1, iced * mean)
    below = zero
    last = zero
    prior = zero
    for l in range(layers):
        visc = row(iv2, l)
        diag = factor * visc + other
        if l == 0:
            diag = diag + iced * bed
        put(td2, l, diag)
        if l < layers - 1:
            face = iced * (2.0 * (visc + row(iv2, l + 1)))
        else:
            face = zero
        inverse = 1.0 / (diag + face + below - below * prior)
        put(inv2, l, inverse)
        put(li2, l, below * inverse)
        prior = face * inverse
        put(pr2, l, prior)
        value = row(v2, l)
        image = diag * value - iced * row(f2, l)
        if l < layers - 1:
            flux = face * (row(v2, l + 1) - value)
            image = image - flux
        else:
            flux = zero
        put(w2, l, image + last)
        last = flux
        below = face
    for l in range(layers):
        scaled = iced * row(iv2, l)
        put(iv2, l, scaled)
        put(x2, l, scaled * row(v2, l))
    for side, s in ((0, 0), (1, 3)):
        smsg[side, 0:layers, :] = gathered(x2, s, layers)
        smsg[side, 24:24 + layers, :] = gathered(x2, s + 4, layers)
        smsg[side, 48:48 + layers, :] = gathered(iv2, s, layers)
        smsg[side, 72:74, :] = gathered(s2, s, 2)
        smsg[side, 74:80, :] = ew[:, s * LANES:(s + 1) * LANES]

    def exchange(parts):
        low, up = me - 1, me + 1

        def copies(side):
            peer = low if side == 0 else up
            return [
                pltpu.make_async_remote_copy(
                    src_ref=src.at[side], dst_ref=dst.at[1 - side],
                    send_sem=ssem.at[side], recv_sem=rsem.at[1 - side],
                    device_id={"region": peer}, device_id_type=MESH,
                )
                for src, dst, ssem, rsem in parts
            ]

        def arrivals(side):
            peer = low if side == 0 else up
            return [
                pltpu.make_async_remote_copy(
                    src_ref=src.at[1 - side], dst_ref=dst.at[side],
                    send_sem=ssem.at[1 - side], recv_sem=rsem.at[side],
                    device_id={"region": peer}, device_id_type=MESH,
                )
                for src, dst, ssem, rsem in parts
            ]

        @pl.when(has_low)
        def _():
            for copy in copies(0):
                copy.start()

        @pl.when(has_up)
        def _():
            for copy in copies(1):
                copy.start()

        def finish(unpack):
            for side, there in ((0, has_low), (1, has_up)):
                @pl.when(there)
                def _():
                    for copy in arrivals(side):
                        copy.wait_recv()
                    unpack(side)

            for side, there in ((0, has_low), (1, has_up)):
                @pl.when(there)
                def _():
                    for copy in copies(side):
                        copy.wait_send()

        return finish

    pl.semaphore_wait(barrier, greeters)
    finish = exchange([(imsg, igot, is_, ir), (smsg, sgot, ss, sr)])
    put(tab, 0, jnp.full((8, LANES), width - REACH, jnp.int32))
    put(tab, 1, jnp.zeros((8, LANES), jnp.int32))

    tab[5:6, :] = imsg[1, NB:NB + 1, :]
    tab[8:9, :] = imsg[0, NB:NB + 1, :]
    h3 = s2.at[pl.ds(16, 16)]
    h3[...] = jnp.zeros((16, LANES), jnp.float32)

    def unpack_first(side):
        s = 0 if side == 0 else 3
        place = 0 if side == 0 else 5
        spread(h2, s, layers, sgot[side, 0:layers, :])
        spread(h2, s + 4, layers, sgot[side, 24:24 + layers, :])
        spread(ivh2, s, layers, sgot[side, 48:48 + layers, :])
        spread(ivh2, s + 4, layers, sgot[side, 48:48 + layers, :])
        spread(h3, place, 2, sgot[side, 72:74, :])
        spread(ewc, place, NB, sgot[side, 74:80, :])
        spread(nbc, place, NB, igot[side, 0:NB, :])
        if side == 0:
            tab[1:2, :] = igot[0, NB:NB + 1, :]
        else:
            tab[12:13, :] = igot[1, NB:NB + 1, :]

    finish(unpack_first)

    middle_rows = (sub >= 1) & (sub <= 4)
    coarse_a = jnp.where(middle_rows, pltpu.roll(row(s2, 0), 1, 0), row(s2, 2))
    coarse_b = jnp.where(middle_rows, pltpu.roll(row(s2, 1), 1, 0), row(s2, 3))
    base = jnp.where(sub == 0, 3 * LANES, jnp.where(sub == 5, 0, (sub - 1) * LANES))
    index_c, high_c, weight_c = [], [], []
    for k in range(NB):
        p = row(nbc, k)
        low_col = pick(row(tab, 0), p & (LANES - 1)) - width
        up_col = pick(row(tab, 1), (p - (width + REACH)) & (LANES - 1)) + width
        col = jnp.where(p < REACH, low_col, jnp.where(p >= width + REACH, up_col, p - REACH))
        rel = col - base
        index_c.append(rel & (LANES - 1))
        high_c.append(rel >= LANES - REACH)
        weight_c.append(row(ewc, k))
        fine = jnp.where(sub < 4, pltpu.roll(rel, 7, 0), pltpu.roll(rel, 3, 0))
        put(idxf, k, fine)
        put(ewf, k, iced * row(ewf, k))

    def near(value, before, after, index, high, weight):
        first = jnp.where(tail, before, value)
        second = jnp.where(tail, value, after)
        acc = None
        for k in range(NB):
            got_k = jnp.where(high[k], pick(second, index[k]), pick(first, index[k]))
            term = weight[k] * got_k
            acc = term if acc is None else acc + term
        return acc

    def near_coarse(value):
        return near(
            value, pltpu.roll(value, 1, 0), pltpu.roll(value, 7, 0), index_c, high_c, weight_c
        )

    first_tile, last_tile = tile == 0, tile == 3

    def near_fine(value, halo):
        before = jnp.where(first_tile, halo, pltpu.roll(value, 1, 0))
        after = jnp.where(last_tile, halo, pltpu.roll(value, 7, 0))
        index, high, weight = [], [], []
        for k in range(NB):
            rel = row(idxf, k)
            index.append(rel & (LANES - 1))
            high.append(rel >= LANES - REACH)
            weight.append(row(ewf, k))
        return near(value, before, after, index, high, weight)

    def first_residual(l, norm):
        at = pl.ds(pl.multiple_of(8 * l, 8), 8)
        resid = w2[at, :] - near_fine(x2[at, :], h2[at, :])
        w2[at, :] = resid
        u2[0, at, :] = -resid
        return norm + resid * resid

    norm = lax.fori_loop(0, layers, first_residual, zero, unroll=True)
    for c in range(2):
        for t in range(4):
            res_out[c, :, t * LANES:(t + 1) * LANES] = gathered(w2, 4 * c + t, layers)

    def flat(value):
        return jnp.sum(value, axis=0, keepdims=True)

    reds = ((red0, rs0, rr0, inner, ia), (red1, rs1, rr1, n // inner, ib))

    def phase_start(phase, tile_value):
        red, rs, rr, group, mine = reds[phase]
        red[mine] = tile_value
        for off in range(1, group):
            spot, peer = partner(phase, off)
            pltpu.make_async_remote_copy(
                src_ref=red.at[mine], dst_ref=red.at[mine],
                send_sem=rs.at[spot], recv_sem=rr.at[mine],
                device_id={"region": peer}, device_id_type=MESH,
            ).start()

    def phase_end(phase):
        red, rs, rr, group, mine = reds[phase]
        copies = []
        for off in range(1, group):
            spot, peer = partner(phase, off)
            copies.append(pltpu.make_async_remote_copy(
                src_ref=red.at[mine], dst_ref=red.at[spot],
                send_sem=rs.at[spot], recv_sem=rr.at[spot],
                device_id={"region": peer}, device_id_type=MESH,
            ))
        for copy in copies:
            copy.wait_recv()
        total = red[0]
        for slot in range(1, group):
            total = total + red[slot]
        for copy in copies:
            copy.wait_send()
        return total

    def wide(value):
        return jnp.broadcast_to(value, (8, LANES))

    def layer_rows(l):
        return pl.ds(pl.multiple_of(8 * l, 8), 8)

    products = {(0, 0): norm}
    for j in range(M):
        uj, zj = u2.at[j], z2.at[j]
        values = [row(uj, 0) * row(inv2, 0)]
        for l in range(1, layers):
            values.append(row(uj, l) * row(inv2, l) + row(li2, l) * values[l - 1])
        solved = values[layers - 1]
        mean = zero
        for l in range(layers - 1, -1, -1):
            if l < layers - 1:
                solved = values[l] + row(pr2, l) * solved
            put(zj, l, solved)
            weighted = row(iv2, l) * solved
            put(x2, l, weighted)
            mean = mean + weighted
        put(x2, layers, mean * (1.0 / layers))
        for side, s in ((0, 0), (1, 3)):
            msg[j, side, 0:layers + 1, :] = gathered(x2, s, layers + 1)
            msg[j, side, 24:25 + layers, :] = gathered(x2, s + 4, layers + 1)
        finish = exchange([(msg.at[j], got.at[j], hs.at[j], hr.at[j])])

        def unpack(side, j=j):
            s = 0 if side == 0 else 3
            spread(h2, s, layers + 1, got[j, side, 0:layers + 1, :])
            spread(h2, s + 4, layers + 1, got[j, side, 24:25 + layers, :])

        finish(unpack)
        own, halo = row(x2, layers), row(h2, layers)
        outer = [
            jnp.where(sub == 0, halo, jnp.where(sub == 5, pltpu.roll(halo, 2, 0), 0.0)),
            jnp.where(
                sub == 0, pltpu.roll(halo, 4, 0), jnp.where(sub == 5, pltpu.roll(halo, 6, 0), 0.0)
            ),
        ]
        result = []
        for c in range(2):
            start = jnp.where(middle_rows, pltpu.roll(own, 1 if c == 0 else 5, 0), outer[c])
            source = near_coarse(start)
            corr = coarse_a * source
            for sweep in range(2):
                corr = 0.2 * corr + coarse_a * (source + near_coarse(coarse_b * corr))
            result.append(corr)
        e0, e1 = result
        corr = jnp.where(sub < 4, pltpu.roll(e0, 7, 0), pltpu.roll(e1, 3, 0))
        corr_halo = jnp.where(
            sub < 4,
            jnp.where(sub == 0, e0, pltpu.roll(e0, 6, 0)),
            jnp.where(sub == 4, pltpu.roll(e1, 4, 0), pltpu.roll(e1, 2, 0)),
        )

        def image(l, carry, j=j, uj=uj, zj=zj, corr=corr, corr_halo=corr_halo):
            at = layer_rows(l)
            zj[at, :] = zj[at, :] + corr
            value = x2[at, :] + iv2[at, :] * corr
            halo = h2[at, :] + ivh2[at, :] * corr_halo
            w = uj[at, :] + td2[at, :] * corr - near_fine(value, halo)
            fresh = w - uj[at, :]
            if j < M - 1:
                u2[j + 1, at, :] = fresh
            out = [carry[i] + u2[i, at, :] * fresh for i in range(j + 1)]
            return tuple(out) + (carry[j + 1] + fresh * fresh,)

        dots = lax.fori_loop(0, layers, image, (zero,) * (j + 2), unroll=True)
        for i in range(j + 2):
            products[i, j + 1] = dots[i]

    pairs = sorted(products)
    tiles = [flat(products[pair]) for pair in pairs] + [jnp.zeros((1, LANES), jnp.float32)]
    phase_start(0, jnp.concatenate(tiles, axis=0))
    phase_start(1, phase_end(0))
    full = jnp.sum(phase_end(1), axis=1, keepdims=True)
    sums = {pair: full[i:i + 1, :] for i, pair in enumerate(pairs)}
    gram_cols = []
    for k in range(M + 1):
        col = zero
        for i in range(M + 1):
            col = jnp.where(sub == i, wide(sums[min(i, k), max(i, k)]), col)
        gram_cols.append(col)

    def weigh(vector, count):
        out = gram_cols[0] * vector[0:1, :]
        for k in range(1, count):
            out = out + gram_cols[k] * vector[k:k + 1, :]
        return out

    sizes = [jnp.sqrt(wide(sums[0, 0]) + 1e-12)]
    hess = []
    vectors = [jnp.where(sub == 0, 1.0 / sizes[0], 0.0)]
    for j in range(M):
        image_c = vectors[j] + pltpu.roll(vectors[j], 1, 0)
        weighed = weigh(image_c, j + 2)
        column = [wide(flat(vectors[i] * weighed)) for i in range(j + 1)]
        for i in range(j + 1):
            image_c = image_c - column[i] * vectors[i]
        square = wide(flat(image_c * weigh(image_c, j + 2)))
        length = jnp.sqrt(jnp.maximum(square, 0.0) + 1e-12)
        hess.append(column)
        sizes.append(length)
        vectors.append(image_c / length)

    def entry(i, j):
        if i <= j:
            return hess[j][i]
        return sizes[i] if i == j + 1 else None

    gram = [[None] * M for _ in range(M)]
    for a in range(M):
        for b in range(a + 1):
            acc = None
            for i in range(min(a, b) + 2):
                left, right = entry(i, a), entry(i, b)
                if left is None or right is None:
                    continue
                term = left * right
                acc = term if acc is None else acc + term
            gram[a][b] = acc
    right = [sizes[0] * hess[j][0] for j in range(M)]
    chol = [[None] * M for _ in range(M)]
    inv_diag = []
    for a in range(M):
        for b in range(a + 1):
            acc = gram[a][b]
            for i in range(b):
                acc = acc - chol[a][i] * chol[b][i]
            if a == b:
                root = jnp.sqrt(acc)
                inv_diag.append(1.0 / root)
            else:
                chol[a][b] = acc * inv_diag[b]
    forward = []
    for a in range(M):
        acc = right[a]
        for i in range(a):
            acc = acc - chol[a][i] * forward[i]
        forward.append(acc * inv_diag[a])
    coeffs = [None] * M
    for a in range(M - 1, -1, -1):
        acc = forward[a]
        for i in range(a + 1, M):
            acc = acc - chol[i][a] * coeffs[i]
        coeffs[a] = acc * inv_diag[a]
    combined = coeffs[0] * vectors[0]
    for j in range(1, M):
        combined = combined + coeffs[j] * vectors[j]
    coeffs = [wide(combined[j:j + 1, :]) for j in range(M)]
    for l in range(layers):
        value = row(v2, l)
        for j in range(M):
            value = value + coeffs[j] * row(z2.at[j], l)
        put(w2, l, value)
    for c in range(2):
        for t in range(4):
            vel_out[c, :, t * LANES:(t + 1) * LANES] = gathered(w2, 4 * c + t, layers)


def body(velocity_start, forcing, rate_factor, basal_drag, edge_weight, nbr_local, send_list, ice_mask):
    n = lax.axis_size("region")
    layers = velocity_start.shape[1]
    full = 8 * layers
    inner = max(g for g in range(1, n + 1) if n % g == 0 and g * g <= n)
    f32, i32 = jnp.float32, jnp.int32
    V, D = pltpu.VMEM, pltpu.SemaphoreType.DMA
    spec = pl.BlockSpec(memory_space=pltpu.VMEM)
    shape = jax.ShapeDtypeStruct(velocity_start.shape, f32)
    field = V((full, LANES), f32)
    return tuple(pl.pallas_call(
        functools.partial(kernel, n, inner, layers),
        out_shape=(shape, shape),
        in_specs=[spec] * 8,
        out_specs=(spec, spec),
        scratch_shapes=[
            field, field, field, field, field, field, field,
            V((full + 8, LANES), f32), V((full + 8, LANES), f32), field, field, V((32, LANES), f32),
            V((M, full, LANES), f32), V((M, full, LANES), f32),
            V((8 * NB, LANES), f32), V((8 * NB, LANES), i32),
            V((8 * NB, LANES), f32), V((8 * NB, LANES), i32), V((16, LANES), i32),
            V((M, 2, 48, LANES), f32), V((M, 2, 48, LANES), f32),
            V((2, 80, LANES), f32), V((2, 80, LANES), f32),
            V((2, 8, LANES), i32), V((2, 8, LANES), i32),
            V((inner, 16, LANES), f32), V((n // inner, 16, LANES), f32),
            D((M, 2)), D((M, 2)), D((2,)), D((2,)), D((2,)), D((2,)), D((inner,)), D((inner,)),
            D((n // inner,)), D((n // inner,)),
        ],
        compiler_params=pltpu.CompilerParams(
            collective_id=0, has_side_effects=True, vmem_limit_bytes=32 * 1024 * 1024
        ),
    )(
        velocity_start, forcing, rate_factor, basal_drag.reshape(4, LANES), edge_weight, nbr_local,
        send_list, ice_mask.reshape(4, LANES),
    ))


def solution(mesh):
    cols = P(None, None, ("ens", "region"))
    in_specs = (
        cols, cols, P(None, ("ens", "region")), P("region"), P(None, "region"), P(None, "region"),
        P(None, "region"), P("region"),
    )
    return jax.shard_map(body, mesh=mesh, in_specs=in_specs, out_specs=(cols, cols), check_vma=False)
```
